256 devices in a mesh: section: 4 (over y), peer: 64 (over x, z, core).
Axes of the slice: x: 4, y: 4, z: 8, core: 2. Of those that a mesh axis runs over, the one named last changes fastest.
Arguments:
- carried: bfloat16 [4, 512, 5120], P('section', 'peer'), may hold values from -6 to 6
- destination: int32 [4, 512, 1], P('section', 'peer'), may hold values from 0 to 63; in each aligned block of 512 rows (0 to 511, 512 to 1023, ..., all dimensions but the last counted through in order) at most 16 rows name the same one
- norm_gain: bfloat16 [4, 5120], P('section'), may hold values from 0.099609375 to 1.8984375
- w_gate: bfloat16 [4, 13824, 5120], P('section', 'peer'), may hold values from -0.078125 to 0.078125
- w_up: bfloat16 [4, 13824, 5120], P('section', 'peer'), may hold values from -0.078125 to 0.078125
- w_down: bfloat16 [4, 13824, 5120], P('section', 'peer'), may hold values from -0.0546875 to 0.0546875
Outputs:
- layer_out: bfloat16 [4, 1024, 5120], P('section', 'peer')
The draws below stay inside these ranges and needn't reach their ends.
Inputs may be any that keep to these rules, and one draw needn't show every extreme that they name: `destination`: in each section at most 16 rows name the same peer, and in some section some peer is named by exactly 16 rows.
All inputs are finite; a program needn't handle non-finite values.
Results may differ from the reference program's by a relative error of at most 0.0048.
Values may be sent and summed in bfloat16 or wider, within the bound.
No kernel may reach another device: no remote copies, remote signals or barrier semaphores. Data moves between devices by JAX's collectives and lax.ppermute only.
A program may use at most 128 MiB of HBM per device.

```python
import math
import jax
import jax.numpy as jnp
import numpy as np
from jax import lax

D = 5120
FF = 13824
SLOTS = 16
N_ROWS = 512
N_SECTION = 4
N_PEER = 64


def block_scale(own_key, dims, cuts, low, top_value):
    factor_of = 1.0
    for dim, shards_of in cuts:
        heights = jax.random.uniform(jax.random.fold_in(jax.random.fold_in(own_key, 6), dim), (shards_of,), jnp.float32, low / len(cuts), top_value / len(cuts))
        factor_of = factor_of * jnp.repeat(jnp.exp(heights), dims[dim] // shards_of).reshape((-1,) + (1,) * (len(dims) - 1 - dim))
    return factor_of


def shared_out(rng, own, number, rows, amount, top, bound, skew):
    order = jax.random.permutation(rng, amount)
    crowded, ordinary = shares(amount, rows * top, bound, skew, True), shares(amount, rows * top, bound, skew, False)
    places = jnp.arange(amount)

    def named(tallies, rotation):
        used = int((tallies > 0).sum())
        fixed = max(1, used // 4)
        shifted = fixed + (places - fixed + rotation * (used - fixed)) % max(1, amount - fixed)
        return jnp.zeros((amount,), jnp.int32).at[order[jnp.where(places < fixed, places, shifted)]].set(jnp.asarray(tallies, jnp.int32))

    tallies = jnp.where(number % 4 == 0, named(crowded, number // 4), named(ordinary, number - number // 4 - 1))
    mixed = jax.random.permutation(jax.random.fold_in(own, 3), amount)
    source_of, receiver = mixed[0:amount // 2 * 2:2], mixed[1:amount // 2 * 2:2]
    margin = jnp.minimum(tallies[source_of] - 1, bound - tallies[receiver]) // 2
    margin = jnp.where((source_of == order[0]) | (receiver == order[0]) | (tallies[receiver] == 0), 0, jnp.maximum(margin, 0))
    shifted = jax.random.randint(jax.random.fold_in(own, 4), (amount // 2,), 0, 1 << 20) % (margin + 1)
    tallies = tallies.at[source_of].add(-shifted).at[receiver].add(shifted)
    members = jnp.searchsorted(jnp.cumsum(tallies), jnp.arange(rows * top), side="right").astype(jnp.int32)
    table = members.reshape(top, rows).T
    table = table[jax.random.permutation(jax.random.fold_in(own, 1), rows)]
    rotation = jax.random.randint(jax.random.fold_in(own, 2), (rows, 1), 0, top)
    return jnp.take_along_axis(table, (jnp.arange(top)[None, :] + rotation) % top, axis=1)


def shares(count, total, reach, slope, full):
    weights = [(1 << 20) // math.isqrt(rank ** slope) + 1 for rank in range(1, count + 1)]
    largest = reach if full else min(reach, max(-(-total // count), total * weights[0] // sum(weights)))
    least = 1 if total - largest >= count - 1 else 0
    counts, rest = [largest] + [least] * (count - 1), total - largest - least * (count - 1)
    while rest > 0:
        candidates = [i for i in range(1, count) if counts[i] < largest] or [i for i in range(1, count) if counts[i] < reach]
        mass, left = sum([weights[i] for i in candidates]), rest
        for i in candidates:
            extra = min(reach - counts[i], max(1, left * weights[i] // mass), rest)
            counts[i] = counts[i] + extra
            rest = rest - extra
    return np.array(counts)


def centred(rng, extent, width, bound, shards=(), kind=jnp.bfloat16):
    drawn = jax.random.normal(rng, extent, jnp.float32) * width
    if len(shards) > 0:
        drawn = block_scale(rng, extent, shards, -0.22, 0.18) * drawn
    return jnp.clip(drawn, min=-bound, max=bound).astype(kind)


def setup_inputs(seed: int = 0) -> dict:
    seeds = jax.random.split(jax.random.key(seed), 7)
    carried = centred(seeds[0], (N_SECTION, N_ROWS, D), 1.0, 6.0, ((0, 4), (1, 64)))
    destination_keys = jax.random.split(jax.random.fold_in(seeds[1], 1), N_SECTION * N_ROWS // N_ROWS)
    destination_turns = jax.random.permutation(jax.random.fold_in(seeds[1], 3), N_SECTION * N_ROWS // N_ROWS)
    destination = jax.vmap(lambda own, number: shared_out(jax.random.fold_in(seeds[1], 2), own, number, N_ROWS, N_PEER, 1, SLOTS, 2))(destination_keys, destination_turns).reshape((N_SECTION, N_ROWS, 1))
    norm_gain = jnp.clip(1.0 + 0.18 * jax.random.normal(seeds[2], (N_SECTION, D), jnp.float32), 0.099609375, 1.8984375).astype(jnp.bfloat16)
    w_gate = centred(seeds[3], (N_SECTION, FF, D), D ** -0.5, 0.078125, ((0, 4), (1, 64)))
    w_up = centred(seeds[4], (N_SECTION, FF, D), D ** -0.5, 0.078125, ((0, 4), (1, 64)))
    w_down = centred(seeds[5], (N_SECTION, FF, D), FF ** -0.5, 0.0546875, ((0, 4), (1, 64)))
    return dict(carried=carried, destination=destination, norm_gain=norm_gain, w_gate=w_gate, w_up=w_up, w_down=w_down)


epsilon = 1e-05

def section_block(packed):
    arrived, dest_rows, gain_row, gate_mat, up_mat, down_mat = packed
    floated = arrived.astype(jnp.float32)
    scale = lax.rsqrt(lax.optimization_barrier(jnp.mean(floated * floated, axis=-1, keepdims=True)) + epsilon)
    normed = (floated * scale * gain_row.astype(jnp.float32)).astype(jnp.bfloat16)
    gate_value = jnp.dot(normed, gate_mat.T, preferred_element_type=jnp.float32)
    up_value = jnp.dot(normed, up_mat.T, preferred_element_type=jnp.float32)
    hidden = (jax.nn.silu(gate_value) * up_value).astype(jnp.bfloat16)
    mixed = (floated + jnp.dot(hidden, down_mat, preferred_element_type=jnp.float32)).astype(jnp.bfloat16)
    dest_flat = dest_rows[:, 0].astype(jnp.int32)
    onehot = (dest_flat[:, None] == jnp.arange(N_PEER, dtype=jnp.int32)[None, :]).astype(jnp.int32)
    rank_row = lax.optimization_barrier(jnp.sum((jnp.cumsum(onehot, axis=0) - onehot) * onehot, axis=1)).astype(jnp.int32)
    position = dest_flat * SLOTS + rank_row
    placed = jnp.zeros((N_PEER * SLOTS, mixed.shape[1]), jnp.bfloat16)
    return placed.at[position].set(mixed)

def reference(carried, destination, norm_gain, w_gate, w_up, w_down):
    arriving = jnp.roll(carried, 1, axis=0)
    return lax.map(section_block, (arriving, destination, norm_gain, w_gate, w_up, w_down))
```

```python
import jax
import jax.numpy as jnp
from jax import lax
from jax.sharding import Mesh
from jax.sharding import PartitionSpec as P

SLOTS = 16
X, Z, CORES, SECTIONS = 4, 8, 2, 4
EPSILON = 1e-05
BF, F32 = jnp.bfloat16, jnp.float32


def shift(array, axis, by):
    n = lax.axis_size(axis)
    return lax.ppermute(array, axis, [(i, (i + by) % n) for i in range(n)])


def handoff(rows, by):
    pairs = [
        (s * X + x, ((s + 1) % SECTIONS) * X + (x + by) % X)
        for s in range(SECTIONS)
        for x in range(X)
    ]
    return lax.ppermute(rows, ("section", "x"), pairs)


def gather_z(block):
    up = down = block
    held = {0: block}
    for step in range(1, Z // 2 + 1):
        up = shift(up, "z", 1)
        held[step] = up
        if step < Z // 2:
            down = shift(down, "z", -1)
            held[Z - step] = down
    return [held[k] for k in range(Z)]


def add(a, b):
    return a.astype(F32) + b.astype(F32)


def in_order(array, axis, here):
    n = array.shape[axis]
    flipped = jnp.flip(array, axis)
    doubled = jnp.concatenate([flipped, flipped], axis)
    return lax.dynamic_slice_in_dim(doubled, n - 1 - here, n, axis)


def body(carried, destination, norm_gain, w_gate, w_up, w_down):
    width = carried.shape[2]
    x, z, core = lax.axis_index("x"), lax.axis_index("z"), lax.axis_index("core")
    rows_each = carried.shape[1]
    total = rows_each * X * Z * CORES
    quarter, eighth = width // X, width // (X * CORES)

    own = [w_gate[0], w_up[0], w_down[0]]
    other = [shift(w, "core", 1) for w in own]

    dest = lax.optimization_barrier(jnp.broadcast_to(destination[0], (rows_each, 128)))
    dest_all = lax.all_gather(dest, ("x", "z", "core"), axis=0, tiled=True)
    dest_all = lax.optimization_barrier(dest_all)[:, 0]
    row = jnp.arange(total, dtype=jnp.int32)
    earlier = (dest_all[:, None] == dest_all[None, :]) & (row[None, :] < row[:, None])
    rank = jnp.sum(earlier.astype(jnp.int32), axis=1)

    line = jnp.concatenate([handoff(carried[0], k) for k in range(X)], axis=0)
    rows = jnp.concatenate(gather_z(line), axis=0)

    floated = rows.astype(F32)
    scale = lax.rsqrt(jnp.mean(floated * floated, axis=-1, keepdims=True) + EPSILON)
    normed = (floated * scale * norm_gain[0].astype(F32)).astype(BF)
    contract = (((1,), (1,)), ((), ()))

    def absolute(array):
        shaped = array.reshape(Z, X, rows_each, array.shape[-1])
        shaped = in_order(in_order(shaped, 0, z), 1, x)
        return shaped.reshape(array.shape)

    def hidden_of(gate_mat, up_mat):
        gate = lax.dot_general(normed, gate_mat, contract, preferred_element_type=F32)
        up = lax.dot_general(normed, up_mat, contract, preferred_element_type=F32)
        return absolute((jax.nn.silu(gate) * up).astype(BF))

    hidden = [hidden_of(own[0], own[1]), hidden_of(other[0], other[1])]
    partial = jnp.dot(hidden[0], own[2], preferred_element_type=F32) + jnp.dot(
        hidden[1], other[2], preferred_element_type=F32
    )

    def part(k):
        return lax.dynamic_slice_in_dim(partial, lax.rem(x + k, X) * quarter, quarter, 1)

    half = quarter // 2
    far = part(2).astype(BF)
    up = shift(far[:, :half], "x", 1)
    down = shift(far[:, half:], "x", -1)
    near = part(1)
    up = jnp.concatenate([add(near[:, :half], up), near[:, half:]], 1).astype(BF)
    up = shift(up, "x", 1)
    near = part(3)
    down = jnp.concatenate([near[:, :half], add(near[:, half:], down)], 1).astype(BF)
    down = shift(down, "x", -1)
    summed = part(0) + up.astype(F32) + down.astype(F32)

    def swap(array):
        mine = lax.dynamic_slice_in_dim(array, core * eighth, eighth, 1)
        theirs = lax.dynamic_slice_in_dim(array, (1 - core) * eighth, eighth, 1)
        theirs = shift(theirs, "core", 1)
        first = jnp.where(core == 0, mine, theirs)
        second = jnp.where(core == 0, theirs, mine)
        return jnp.concatenate([first, second], 0)

    summed = swap(summed).astype(BF)
    residual = swap(absolute(lax.dynamic_slice_in_dim(rows, x * quarter, quarter, 1)))

    def by_core(per_row):
        return per_row.reshape(X, Z, CORES, rows_each).transpose(2, 1, 0, 3).reshape(total)

    dest_of, rank_of = by_core(dest_all), by_core(rank)
    slots = X * CORES * SLOTS
    dest_z = (dest_of // CORES) % Z
    slot_of = ((dest_of // (CORES * Z)) * CORES + dest_of % CORES) * SLOTS + rank_of
    slot = jnp.arange(slots, dtype=jnp.int32)

    def pick(k):
        at = lax.rem(z + k, Z)
        return ((slot_of[None, :] == slot[:, None]) & (dest_z == at)[None, :]).astype(BF)

    def slotted(k):
        return jnp.dot(pick(k), summed, preferred_element_type=F32)

    up = slotted(Z // 2)
    for k in range(Z // 2 - 1, -1, -1):
        up = shift(up.astype(BF), "z", 1)
        if k:
            up = add(slotted(k), up)
    down = slotted(Z // 2 + 1)
    for k in range(Z // 2 + 2, Z + 1):
        down = shift(down.astype(BF), "z", -1)
        if k < Z:
            down = add(slotted(k), down)
    mine = slotted(0) + jnp.dot(pick(0), residual, preferred_element_type=F32)
    mixed = (mine + up.astype(F32) + down.astype(F32)).astype(BF)

    pieces = lax.all_to_all(
        mixed.reshape(X * CORES, SLOTS, eighth), ("x", "core"), 0, 0, tiled=True
    )
    return pieces.transpose(1, 0, 2).reshape(1, SLOTS, width)


def solution(mesh):
    split = Mesh(
        mesh.devices.reshape(SECTIONS, X, Z, CORES), ("section", "x", "z", "core")
    )
    peers = ("x", "z", "core")
    return jax.shard_map(
        body,
        mesh=split,
        in_specs=(
            P("section", peers, None),
            P("section", peers, None),
            P("section", None),
            P("section", peers, None),
            P("section", peers, None),
            P("section", peers, None),
        ),
        out_specs=P("section", peers, None),
        check_vma=False,
    )
```

```python
import jax
import jax.numpy as jnp
from jax import lax
from jax.sharding import Mesh
from jax.sharding import PartitionSpec as P

SLOTS = 16
X, Z, CORES, SECTIONS = 4, 8, 2, 4
LANES = 128
EPSILON = 1e-05
BF, F32 = jnp.bfloat16, jnp.float32
FIRST, LAST = (0, 1, 7, 2, 6), (3, 5, 4)


def shift(array, axis, by):
    n = lax.axis_size(axis)
    return lax.ppermute(array, axis, [(i, (i + by) % n) for i in range(n)])


def handoff(rows, by):
    pairs = [
        (s * X + x, ((s + 1) % SECTIONS) * X + (x + by) % X)
        for s in range(SECTIONS)
        for x in range(X)
    ]
    return lax.ppermute(rows, ("section", "x"), pairs)


def gather_z(block):
    up = down = block
    held = {0: block}
    for step in range(1, Z // 2 + 1):
        up = shift(up, "z", 1)
        held[step] = up
        if step < Z // 2:
            down = shift(down, "z", -1)
            held[Z - step] = down
    return held


def add(a, b):
    return a.astype(F32) + b.astype(F32)


def body(carried, destination, norm_gain, w_gate, w_up, w_down):
    width = carried.shape[2]
    x, z, core = lax.axis_index("x"), lax.axis_index("z"), lax.axis_index("core")
    rows_each = carried.shape[1]
    total = rows_each * X * Z * CORES
    quarter, eighth = width // X, width // (X * CORES)

    def pair(own):
        return jnp.concatenate([own, shift(own, "core", 1)], 0)

    gate_mat, up_mat, down_mat = pair(w_gate[0]), pair(w_up[0]), pair(w_down[0])
    down_part = [
        lax.dynamic_slice_in_dim(down_mat, lax.rem(x + k, X) * quarter, quarter, 1)
        for k in range(X)
    ]

    line = jnp.zeros((X * rows_each, width + LANES), BF)
    for k in range(X):
        line = lax.dynamic_update_slice(
            line, handoff(carried[0], k), (lax.rem(x + X - k, X) * rows_each, 0)
        )
    dest = jnp.broadcast_to(destination[0].astype(BF), (rows_each, LANES))
    line = lax.dynamic_update_slice(line, dest, (0, width))
    held = gather_z(line)

    gain = norm_gain[0].astype(F32)
    contract = (((1,), (1,)), ((), ()))

    def hidden_of(order):
        floated = jnp.concatenate([held[k] for k in order], 0)[:, :width].astype(F32)
        scale = lax.rsqrt(jnp.mean(floated * floated, axis=-1, keepdims=True) + EPSILON)
        normed = (floated * scale * gain).astype(BF)
        gate = lax.dot_general(normed, gate_mat, contract, preferred_element_type=F32)
        up = lax.dot_general(normed, up_mat, contract, preferred_element_type=F32)
        return (jax.nn.silu(gate) * up).astype(BF)

    hidden = jnp.concatenate([hidden_of(FIRST), hidden_of(LAST)], 0)
    order = FIRST + LAST

    def part(k):
        return jnp.dot(hidden, down_part[k], preferred_element_type=F32)

    half = quarter // 2
    far = part(2).astype(BF)
    up = shift(far[:, :half], "x", 1)
    down = shift(far[:, half:], "x", -1)
    near = part(1)
    up = jnp.concatenate([add(near[:, :half], up), near[:, half:]], 1).astype(BF)
    up = shift(up, "x", 1)
    near = part(3)
    down = jnp.concatenate([near[:, :half], add(near[:, half:], down)], 1).astype(BF)
    down = shift(down, "x", -1)
    summed = part(0) + up.astype(F32) + down.astype(F32)

    def swap(array):
        mine = lax.dynamic_slice_in_dim(array, core * eighth, eighth, 1)
        theirs = lax.dynamic_slice_in_dim(array, (1 - core) * eighth, eighth, 1)
        return jnp.concatenate([mine, shift(theirs, "core", 1)], 0)

    kept = jnp.concatenate([held[k][:, :width] for k in order], 0)
    residual = swap(lax.dynamic_slice_in_dim(kept, x * quarter, quarter, 1))

    dest = jnp.concatenate([held[k][:rows_each, width:] for k in order], 0)
    dests = jnp.zeros((X,) + dest.shape, BF)
    for k in range(X):
        there = shift(dest, "x", k) if k else dest
        dests = lax.dynamic_update_slice(dests, there[None], (lax.rem(x + X - k, X), 0, 0))
    dests = dests.reshape(X, Z, rows_each, LANES).transpose(1, 0, 2, 3)
    dests = dests.reshape(total // CORES, LANES)
    dest = jnp.concatenate([dests, shift(dests, "core", 1)], 0)[:, 0].astype(jnp.int32)
    index = jnp.arange(total, dtype=jnp.int32)
    block = (index // (X * rows_each)) % Z
    behind = jnp.zeros_like(block)
    for i, k in enumerate(order):
        behind = jnp.where(block == i, k, behind)
    source_core = jnp.where(index < total // CORES, core, 1 - core)
    source = ((index // rows_each) % X) * Z + lax.rem(z + Z - behind, Z)
    key = (source * CORES + source_core) * rows_each + index % rows_each
    earlier = (dest[:, None] == dest[None, :]) & (key[None, :] < key[:, None])
    rank = jnp.sum(earlier.astype(jnp.int32), axis=1)

    summed = swap(summed).astype(BF)

    slots = X * CORES * SLOTS
    dest_z = (dest // CORES) % Z
    slot_of = ((dest // (CORES * Z)) * CORES + dest % CORES) * SLOTS + rank
    slot = jnp.arange(slots, dtype=jnp.int32)

    def pick(k):
        at = lax.rem(z + k, Z)
        return ((slot_of[None, :] == slot[:, None]) & (dest_z == at)[None, :]).astype(BF)

    def slotted(k):
        return jnp.dot(pick(k), summed, preferred_element_type=F32)

    up = slotted(Z // 2)
    for k in range(Z // 2 - 1, -1, -1):
        up = shift(up.astype(BF), "z", 1)
        if k:
            up = add(slotted(k), up)
    down = slotted(Z // 2 + 1)
    for k in range(Z // 2 + 2, Z + 1):
        down = shift(down.astype(BF), "z", -1)
        if k < Z:
            down = add(slotted(k), down)
    mine = slotted(0) + jnp.dot(pick(0), residual, preferred_element_type=F32)
    mixed = (mine + up.astype(F32) + down.astype(F32)).astype(BF)

    pieces = lax.all_to_all(
        mixed.reshape(X * CORES, SLOTS, eighth), ("x", "core"), 0, 0, tiled=True
    )
    return pieces.transpose(1, 0, 2).reshape(1, SLOTS, width)


def solution(mesh):
    split = Mesh(
        mesh.devices.reshape(SECTIONS, X, Z, CORES), ("section", "x", "z", "core")
    )
    peers = ("x", "z", "core")
    return jax.shard_map(
        body,
        mesh=split,
        in_specs=(
            P("section", peers, None),
            P("section", peers, None),
            P("section", None),
            P("section", peers, None),
            P("section", peers, None),
            P("section", peers, None),
        ),
        out_specs=P("section", peers, None),
        check_vma=False,
    )
```

```python
import jax
import jax.numpy as jnp
from jax import lax
from jax.sharding import Mesh
from jax.sharding import PartitionSpec as P

SLOTS = 16
X, Z, CORES, SECTIONS = 4, 8, 2, 4
LANES = 128
EPSILON = 1e-05
BF, F32 = jnp.bfloat16, jnp.float32
ORDER = (0, 1, 7, 2, 6, 3, 5, 4)


def shift(array, axis, by):
    n = lax.axis_size(axis)
    return lax.ppermute(array, axis, [(i, (i + by) % n) for i in range(n)])


def handoff(rows, by):
    pairs = [
        (s * X + x, ((s + 1) % SECTIONS) * X + (x + by) % X)
        for s in range(SECTIONS)
        for x in range(X)
    ]
    return lax.ppermute(rows, ("section", "x"), pairs)


def gather_z(blocks):
    ups, downs = list(blocks), list(blocks)
    held = {0: list(blocks)}
    for step in range(1, Z // 2 + 1):
        for i in range(len(blocks)):
            ups[i] = shift(ups[i], "z", 1)
            if step < Z // 2:
                downs[i] = shift(downs[i], "z", -1)
        held[step] = list(ups)
        if step < Z // 2:
            held[Z - step] = list(downs)
    return [jnp.concatenate([held[k][i] for k in ORDER], 0) for i in range(len(blocks))]


def add(a, b):
    return a.astype(F32) + b.astype(F32)


def body(carried, destination, norm_gain, w_gate, w_up, w_down):
    width = carried.shape[2]
    x, z, core = lax.axis_index("x"), lax.axis_index("z"), lax.axis_index("core")
    rows_each = carried.shape[1]
    total = rows_each * X * Z * CORES
    quarter, eighth = width // X, width // (X * CORES)

    def pair(own):
        return jnp.concatenate([own, shift(own, "core", 1)], 0)

    gate_mat, up_mat, down_mat = pair(w_gate[0]), pair(w_up[0]), pair(w_down[0])
    down_part = [
        lax.dynamic_slice_in_dim(down_mat, lax.rem(x + k, X) * quarter, quarter, 1)
        for k in range(X)
    ]

    came = [handoff(carried[0], k) for k in range(X)]
    line = [lax.select_n(lax.rem(x + X - j, X), *came) for j in range(X)]
    dest = jnp.broadcast_to(destination[0].astype(BF), (rows_each, LANES))
    dest = jnp.concatenate([dest, jnp.zeros(((X - 1) * rows_each, LANES), BF)], 0)
    line = jnp.concatenate(line, 0)
    left = jnp.concatenate([line[:, : width // 2], dest], 1)
    left, right = gather_z([left, line[:, width // 2 :]])
    dest = left.reshape(Z, X * rows_each, -1)[:, :rows_each, width // 2 :]
    rows = jnp.concatenate([left[:, : width // 2], right], 1)

    gain = norm_gain[0].astype(F32)
    contract = (((1,), (1,)), ((), ()))
    floated = rows.astype(F32)
    scale = lax.rsqrt(jnp.mean(floated * floated, axis=-1, keepdims=True) + EPSILON)
    normed = (floated * scale * gain).astype(BF)
    gate = lax.dot_general(normed, gate_mat, contract, preferred_element_type=F32)
    up = lax.dot_general(normed, up_mat, contract, preferred_element_type=F32)
    hidden = (jax.nn.silu(gate) * up).astype(BF)

    def part(k):
        return jnp.dot(hidden, down_part[k], preferred_element_type=F32)

    half = quarter // 2
    far = part(2).astype(BF)
    far, dest = lax.optimization_barrier((far, dest))
    up = shift(far[:, :half], "x", 1)
    down = shift(far[:, half:], "x", -1)
    near = part(1)
    up = jnp.concatenate([add(near[:, :half], up), near[:, half:]], 1).astype(BF)
    up = shift(up, "x", 1)
    near = part(3)
    down = jnp.concatenate([near[:, :half], add(near[:, half:], down)], 1).astype(BF)
    down = shift(down, "x", -1)
    summed = part(0) + up.astype(F32) + down.astype(F32)

    def swap(array):
        mine = lax.dynamic_slice_in_dim(array, core * eighth, eighth, 1)
        theirs = lax.dynamic_slice_in_dim(array, (1 - core) * eighth, eighth, 1)
        return jnp.concatenate([mine, shift(theirs, "core", 1)], 0)

    residual = swap(lax.dynamic_slice_in_dim(rows, x * quarter, quarter, 1))

    dests = jnp.zeros((X,) + dest.shape, BF)
    for k in range(X):
        there = shift(dest, "x", k) if k else dest
        dests = lax.dynamic_update_slice(
            dests, there[None], (lax.rem(x + X - k, X), 0, 0, 0)
        )
    dests = dests.transpose(1, 0, 2, 3)
    dests = dests.reshape(total // CORES, LANES)
    dest = jnp.concatenate([dests, shift(dests, "core", 1)], 0)[:, 0].astype(jnp.int32)
    index = jnp.arange(total, dtype=jnp.int32)
    block = (index // (X * rows_each)) % Z
    behind = jnp.zeros_like(block)
    for i, k in enumerate(ORDER):
        behind = jnp.where(block == i, k, behind)
    source_core = jnp.where(index < total // CORES, core, 1 - core)
    source = ((index // rows_each) % X) * Z + lax.rem(z + Z - behind, Z)
    key = (source * CORES + source_core) * rows_each + index % rows_each
    earlier = (dest[:, None] == dest[None, :]) & (key[None, :] < key[:, None])
    rank = jnp.sum(earlier.astype(jnp.int32), axis=1)

    summed = swap(summed).astype(BF)

    slots = X * CORES * SLOTS
    dest_z = (dest // CORES) % Z
    slot_of = ((dest // (CORES * Z)) * CORES + dest % CORES) * SLOTS + rank
    slot = jnp.arange(slots, dtype=jnp.int32)

    def pick(k):
        at = lax.rem(z + k, Z)
        return ((slot_of[None, :] == slot[:, None]) & (dest_z == at)[None, :]).astype(BF)

    def slotted(k):
        return jnp.dot(pick(k), summed, preferred_element_type=F32)

    def message(*steps):
        return jnp.concatenate([slotted(k % Z).astype(BF) for k in steps], 0)

    middle = slots // 2
    up_near = shift(message(3, 1), "z", 1)
    down_near = shift(message(-3, -1), "z", -1)
    opposite = message(4)
    up_far = shift(opposite[:middle], "z", 2)
    down_far = shift(opposite[middle:], "z", -2)
    up = add(slotted(2), up_near[:slots])
    up = jnp.concatenate([add(up[:middle], up_far), up[middle:]], 0)
    down = add(slotted(6), down_near[:slots])
    down = jnp.concatenate([down[:middle], add(down[middle:], down_far)], 0)
    up = shift(up.astype(BF), "z", 2)
    down = shift(down.astype(BF), "z", -2)
    mine = slotted(0) + jnp.dot(pick(0), residual, preferred_element_type=F32)
    near = add(up_near[slots:], down_near[slots:])
    mixed = (mine + near + add(up, down)).astype(BF)

    pieces = lax.all_to_all(
        mixed.reshape(X * CORES, SLOTS, eighth), ("x", "core"), 0, 0, tiled=True
    )
    return pieces.transpose(1, 0, 2).reshape(1, SLOTS, width)


def solution(mesh):
    split = Mesh(
        mesh.devices.reshape(SECTIONS, X, Z, CORES), ("section", "x", "z", "core")
    )
    peers = ("x", "z", "core")
    return jax.shard_map(
        body,
        mesh=split,
        in_specs=(
            P("section", peers, None),
            P("section", peers, None),
            P("section", None),
            P("section", peers, None),
            P("section", peers, None),
            P("section", peers, None),
        ),
        out_specs=P("section", peers, None),
        check_vma=False,
    )
```

```python
import jax
import jax.numpy as jnp
from jax import lax
from jax.sharding import Mesh
from jax.sharding import PartitionSpec as P

SLOTS = 16
X, Z, CORES, SECTIONS = 4, 8, 2, 4
LANES = 128
EPSILON = 1e-05
BF, F32 = jnp.bfloat16, jnp.float32
ORDER = (0, 1, -1, 2, -2, 3, -3, 4)


def shift(array, axis, by):
    n = lax.axis_size(axis)
    return lax.ppermute(array, axis, [(i, (i + by) % n) for i in range(n)])


def handoff(rows, by):
    pairs = [
        (s * Z + z, ((s + 1) % SECTIONS) * Z + (z + by) % Z)
        for s in range(SECTIONS)
        for z in range(Z)
    ]
    return lax.ppermute(rows, ("section", "z"), pairs)


def gather_z(rows):
    came = {k: handoff(rows, k) for k in (0, 1, -1, 2, -2)}
    came[3] = shift(came[2], "z", 1)
    came[-3] = shift(came[-2], "z", -1)
    came[4] = shift(came[2], "z", 2)
    return jnp.concatenate([came[k] for k in ORDER], 0)


def gather_x(block, x):
    size = block.shape[0]
    half = size // 2
    up, down = shift(block, "x", 1), shift(block, "x", -1)
    far_up, far_down = shift(up[:half], "x", 1), shift(down[half:], "x", -1)
    rows = jnp.zeros((X * size, block.shape[1]), block.dtype)
    for part, behind, offset in (
        (block, 0, 0),
        (up, 1, 0),
        (down, 3, 0),
        (far_up, 2, 0),
        (far_down, 2, half),
    ):
        at = lax.rem(x + X - behind, X) * size + offset
        rows = lax.dynamic_update_slice_in_dim(rows, part, at, 0)
    return rows


def add(a, b):
    return a.astype(F32) + b.astype(F32)


def body(carried, destination, norm_gain, w_gate, w_up, w_down):
    width = carried.shape[2]
    x, z, core = lax.axis_index("x"), lax.axis_index("z"), lax.axis_index("core")
    rows_each = carried.shape[1]
    total = rows_each * X * Z * CORES
    quarter, eighth = width // X, width // (X * CORES)

    def pair(own):
        return jnp.concatenate([own, shift(own, "core", 1)], 0)

    gate_mat, up_mat, down_mat = pair(w_gate[0]), pair(w_up[0]), pair(w_down[0])
    down_part = [
        lax.dynamic_slice_in_dim(down_mat, lax.rem(x + k, X) * quarter, quarter, 1)
        for k in range(X)
    ]

    dest = jnp.broadcast_to(destination[0].astype(BF), (rows_each, LANES))
    other_dest = shift(dest, "core", 1)
    dest = [jnp.where(core == 0, dest, other_dest), jnp.where(core == 0, other_dest, dest)]
    dest.append(jnp.zeros(((Z - CORES) * rows_each, LANES), BF))
    block = jnp.concatenate([gather_z(carried[0]), jnp.concatenate(dest, 0)], 1)
    rows = gather_x(block, x)
    dest = rows.reshape(X, Z * rows_each, -1)[:, : CORES * rows_each, width:]
    rows = rows[:, :width]
    behind_1 = shift(dest, "z", 1)

    gain = norm_gain[0].astype(F32)
    contract = (((1,), (1,)), ((), ()))
    floated = rows.astype(F32)
    scale = lax.rsqrt(jnp.mean(floated * floated, axis=-1, keepdims=True) + EPSILON)
    normed = (floated * scale * gain).astype(BF)
    gate = lax.dot_general(normed, gate_mat, contract, preferred_element_type=F32)
    up = lax.dot_general(normed, up_mat, contract, preferred_element_type=F32)
    hidden = (jax.nn.silu(gate) * up).astype(BF)

    def part(k):
        return jnp.dot(hidden, down_part[k], preferred_element_type=F32)

    half = quarter // 2
    far, dest, behind_1 = lax.optimization_barrier((part(2).astype(BF), dest, behind_1))
    up = shift(far[:, :half], "x", 1)
    down = shift(far[:, half:], "x", -1)
    dest = jnp.stack([dest, behind_1])
    near_up, near_down, dest = lax.optimization_barrier((part(1), part(3), dest))
    behind_2 = shift(dest, "z", 2)
    up, down, dest, behind_2 = lax.optimization_barrier((up, down, dest, behind_2))
    up = jnp.concatenate([add(near_up[:, :half], up), near_up[:, half:]], 1).astype(BF)
    up = shift(up, "x", 1)
    down = jnp.concatenate([near_down[:, :half], add(near_down[:, half:], down)], 1)
    down = shift(down.astype(BF), "x", -1)
    kept, dest = lax.optimization_barrier((part(0), jnp.concatenate([dest, behind_2], 0)))
    dest = jnp.concatenate([dest, shift(dest, "z", 4)], 0)
    summed = kept + up.astype(F32) + down.astype(F32)

    def swap(array):
        mine = lax.dynamic_slice_in_dim(array, core * eighth, eighth, 1)
        theirs = lax.dynamic_slice_in_dim(array, (1 - core) * eighth, eighth, 1)
        return jnp.concatenate([mine, shift(theirs, "core", 1)], 0)

    residual = swap(lax.dynamic_slice_in_dim(rows, x * quarter, quarter, 1))

    dest = jnp.stack([dest[k % Z] for k in ORDER]).reshape(Z, X, CORES, rows_each, LANES)
    dest = dest.transpose(2, 1, 0, 3, 4)
    dest = jnp.where(core == 0, dest, dest[::-1])
    dest = dest.reshape(total, LANES)[:, 0].astype(jnp.int32)
    index = jnp.arange(total, dtype=jnp.int32)
    place_z = (index // rows_each) % Z
    behind = jnp.zeros_like(index)
    for i, k in enumerate(ORDER):
        behind = jnp.where(place_z == i, k, behind)
    source_core = jnp.where(index < total // CORES, core, 1 - core)
    source_x = (index // (rows_each * Z)) % X
    source = source_x * Z + lax.rem(z + Z - behind, Z)
    key = (source * CORES + source_core) * rows_each + index % rows_each
    earlier = (dest[:, None] == dest[None, :]) & (key[None, :] < key[:, None])
    rank = jnp.sum(earlier.astype(jnp.int32), axis=1)

    summed = swap(summed).astype(BF)

    slots = X * CORES * SLOTS
    dest_z = (dest // CORES) % Z
    slot_of = ((dest // (CORES * Z)) * CORES + dest % CORES) * SLOTS + rank
    slot = jnp.arange(slots, dtype=jnp.int32)

    def pick(k):
        at = lax.rem(z + k, Z)
        return ((slot_of[None, :] == slot[:, None]) & (dest_z == at)[None, :]).astype(BF)

    def slotted(k):
        return jnp.dot(pick(k), summed, preferred_element_type=F32)

    def message(*steps):
        return jnp.concatenate([slotted(k % Z).astype(BF) for k in steps], 0)

    middle = slots // 2
    up_near = shift(message(3, 1), "z", 1)
    down_near = shift(message(-3, -1), "z", -1)
    opposite = message(4)
    up_far = shift(opposite[:middle], "z", 2)
    down_far = shift(opposite[middle:], "z", -2)
    up = add(slotted(2), up_near[:slots])
    up = jnp.concatenate([add(up[:middle], up_far), up[middle:]], 0)
    down = add(slotted(6), down_near[:slots])
    down = jnp.concatenate([down[:middle], add(down[middle:], down_far)], 0)
    up = shift(up.astype(BF), "z", 2)
    down = shift(down.astype(BF), "z", -2)
    mine = slotted(0) + jnp.dot(pick(0), residual, preferred_element_type=F32)
    near = add(up_near[slots:], down_near[slots:])
    mixed = (mine + near + add(up, down)).astype(BF)

    pieces = lax.all_to_all(
        mixed.reshape(X * CORES, SLOTS, eighth), ("x", "core"), 0, 0, tiled=True
    )
    return pieces.transpose(1, 0, 2).reshape(1, SLOTS, width)


def solution(mesh):
    split = Mesh(
        mesh.devices.reshape(SECTIONS, X, Z, CORES), ("section", "x", "z", "core")
    )
    peers = ("x", "z", "core")
    return jax.shard_map(
        body,
        mesh=split,
        in_specs=(
            P("section", peers, None),
            P("section", peers, None),
            P("section", None),
            P("section", peers, None),
            P("section", peers, None),
            P("section", peers, None),
        ),
        out_specs=P("section", peers, None),
        check_vma=False,
    )
```

```python
import jax
import jax.numpy as jnp
from jax import lax
from jax.experimental import pallas as pl
from jax.experimental.pallas import tpu as pltpu
from jax.sharding import Mesh
from jax.sharding import PartitionSpec as P

SLOTS = 16
X, Z, CORES, SECTIONS = 4, 8, 2, 4
LANES = 128
VMEM = 32 * 1024 * 1024
EPSILON = 1e-05
BF, F32 = jnp.bfloat16, jnp.float32
ORDER = (0, 1, -1, 2, -2, 3, -3, 4)


def shift(array, axis, by):
    n = lax.axis_size(axis)
    return lax.ppermute(array, axis, [(i, (i + by) % n) for i in range(n)])


def handoff(rows, by):
    pairs = [
        (s * Z + z, ((s + 1) % SECTIONS) * Z + (z + by) % Z)
        for s in range(SECTIONS)
        for z in range(Z)
    ]
    return lax.ppermute(rows, ("section", "z"), pairs)


def gather_z(rows, dest):
    back = lax.ppermute(dest, "section", [(s, (s - 1) % SECTIONS) for s in range(SECTIONS)])
    first = handoff(rows, 0)
    rows = labelled(rows, back)
    came = {k: handoff(rows, k) for k in (2, -2, 1, -1)}
    came[0] = labelled(first, dest)
    came[3] = shift(came[2], "z", 1)
    came[-3] = shift(came[-2], "z", -1)
    came[4] = shift(came[2], "z", 2)
    return jnp.concatenate([came[k] for k in ORDER], 0)


def labelled(rows, dest):
    lanes = jnp.broadcast_to(dest.astype(BF), (rows.shape[0], LANES))
    return jnp.concatenate([rows, lanes], 1)


def norm_rows(rows, gain):
    floated = rows.astype(F32)
    scale = lax.rsqrt(jnp.mean(floated * floated, axis=-1, keepdims=True) + EPSILON)
    return (floated * scale * gain).astype(BF)


def norm_kernel(a_ref, b_ref, c_ref, gain_ref, out_ref):
    width = gain_ref.shape[1]
    gain = gain_ref[...].astype(F32)
    for i, ref in enumerate((a_ref, b_ref, c_ref)):
        size = ref.shape[0]
        out_ref[i * size : (i + 1) * size, :] = norm_rows(ref[:, :width], gain)


def normed_of(blocks, gain):
    size, width = blocks[0].shape[0], gain.shape[1]
    return pl.pallas_call(
        norm_kernel,
        out_shape=jax.ShapeDtypeStruct((len(blocks) * size, width), BF),
        compiler_params=pltpu.CompilerParams(vmem_limit_bytes=VMEM),
        cost_estimate=pl.CostEstimate(
            flops=15 * size * width, bytes_accessed=12 * size * width, transcendentals=0
        ),
    )(*blocks, gain)


def hidden_kernel(
    x_ref, normed_ref, far_up_ref, far_down_ref, gain_ref, gate_0, up_0, gate_1, up_1,
    down_0, down_1, hidden_0, hidden_1, far_ref, rows, far_rows, sums,
):
    step, steps = pl.program_id(0), pl.num_programs(0)
    width, part = gain_ref.shape[1], normed_ref.shape[1]
    size = far_rows.shape[0]
    half = size // 2

    @pl.when(step == 0)
    def _():
        gain = gain_ref[...].astype(F32)
        far_rows[:half, :] = norm_rows(far_up_ref[:, :width], gain)
        far_rows[half:, :] = norm_rows(far_down_ref[:, :width], gain)
        sums[...] = jnp.zeros_like(sums)

    rows[: 3 * size, :] = normed_ref[...]
    rows[3 * size :, :] = far_rows[:, pl.ds(pl.multiple_of(step * part, part), part)]
    contract = (((1,), (1,)), ((), ()))
    for i, weight in enumerate((gate_0, up_0, gate_1, up_1)):
        sums[i] += lax.dot_general(
            rows[...], weight[...], contract, preferred_element_type=F32
        )

    @pl.when(step == steps - 1)
    def _():
        for i, hidden in enumerate((hidden_0, hidden_1)):
            value = (jax.nn.silu(sums[2 * i]) * sums[2 * i + 1]).astype(BF)
            for j, behind in enumerate((0, 1, 3, 2)):
                at = lax.rem(x_ref[0] + X - behind, X) * size
                hidden[pl.ds(pl.multiple_of(at, size), size), :] = value[j * size : (j + 1) * size]
        far_ref[...] = (
            jnp.dot(hidden_0[...], down_0[...], preferred_element_type=F32)
            + jnp.dot(hidden_1[...], down_1[...], preferred_element_type=F32)
        ).astype(BF)


def hidden_of(x, normed, far_up, far_down, gain, gates, ups, downs):
    units, width = gates[0].shape
    size, part = 2 * far_up.shape[0], width // X
    total = X * size
    whole = lambda array: pl.BlockSpec(array.shape, lambda i, x: (0, 0))
    weight = pl.BlockSpec((units, part), lambda i, x: (0, i))
    down = pl.BlockSpec((units, part), lambda i, x: (0, lax.rem(x[0] + 2, X)))
    hidden = jax.ShapeDtypeStruct((total, units), BF)
    return pl.pallas_call(
        hidden_kernel,
        grid_spec=pltpu.PrefetchScalarGridSpec(
            num_scalar_prefetch=1,
            grid=(X,),
            in_specs=[
                pl.BlockSpec((3 * size, part), lambda i, x: (0, i)),
                whole(far_up), whole(far_down), whole(gain),
                weight, weight, weight, weight, down, down,
            ],
            out_specs=[
                pl.BlockSpec((total, units), lambda i, x: (0, 0)),
                pl.BlockSpec((total, units), lambda i, x: (0, 0)),
                pl.BlockSpec((total, part), lambda i, x: (0, 0)),
            ],
            scratch_shapes=[
                pltpu.VMEM((total, part), BF),
                pltpu.VMEM((size, width), BF),
                pltpu.VMEM((4, total, units), F32),
            ],
        ),
        out_shape=[hidden, hidden, jax.ShapeDtypeStruct((total, part), BF)],
        compiler_params=pltpu.CompilerParams(vmem_limit_bytes=VMEM),
        cost_estimate=pl.CostEstimate(
            flops=9 * total * units * width, bytes_accessed=10 * units * width, transcendentals=0
        ),
    )(x, normed, far_up, far_down, gain, gates[0], ups[0], gates[1], ups[1], *downs)


def part_kernel(x_ref, hidden_0, hidden_1, down_0, down_1, out_ref):
    out_ref[0] = jnp.dot(
        hidden_0[...], down_0[...], preferred_element_type=F32
    ) + jnp.dot(hidden_1[...], down_1[...], preferred_element_type=F32)


def parts_of(x, hiddens, downs):
    units, width = downs[0].shape
    total, part = hiddens[0].shape[0], width // X
    hidden = pl.BlockSpec((total, units), lambda i, x: (0, 0))
    quarter = lambda i, x: (0, lax.rem(x[0] + lax.rem(2 * i + 1, 5), X))
    down = pl.BlockSpec((units, part), quarter)
    return pl.pallas_call(
        part_kernel,
        grid_spec=pltpu.PrefetchScalarGridSpec(
            num_scalar_prefetch=1,
            grid=(3,),
            in_specs=[hidden, hidden, down, down],
            out_specs=pl.BlockSpec((1, total, part), lambda i, x: (i, 0, 0)),
        ),
        out_shape=jax.ShapeDtypeStruct((3, total, part), F32),
        compiler_params=pltpu.CompilerParams(vmem_limit_bytes=VMEM),
        cost_estimate=pl.CostEstimate(
            flops=3 * total * units * width, bytes_accessed=6 * units * width, transcendentals=0
        ),
    )(x, *hiddens, *downs)


def add(a, b):
    return a.astype(F32) + b.astype(F32)


def body(carried, destination, norm_gain, w_gate, w_up, w_down):
    width = carried.shape[2]
    x, z, core = lax.axis_index("x"), lax.axis_index("z"), lax.axis_index("core")
    rows_each = carried.shape[1]
    total = rows_each * X * Z * CORES
    quarter, eighth = width // X, width // (X * CORES)

    gates, ups, downs = (
        [w[0], shift(w[0], "core", 1)] for w in (w_gate, w_up, w_down)
    )
    at_x = x.astype(jnp.int32)[None]

    block = gather_z(carried[0], destination[0])
    size = block.shape[0]
    up, down = shift(block, "x", 1), shift(block, "x", -1)
    far_up, far_down = shift(up[: size // 2], "x", 1), shift(down[size // 2 :], "x", -1)
    normed = normed_of([block, up, down], norm_gain)
    *hiddens, far = hidden_of(
        at_x, normed, far_up, far_down, norm_gain, gates, ups, downs
    )

    rows = jnp.zeros((X * size, quarter + LANES), BF)
    for piece, behind, offset in (
        (block, 0, 0),
        (up, 1, 0),
        (down, 3, 0),
        (far_up, 2, 0),
        (far_down, 2, size // 2),
    ):
        at = lax.rem(x + X - behind, X) * size + offset
        kept = lax.dynamic_slice_in_dim(piece, x * quarter, quarter, 1)
        kept = jnp.concatenate([kept, piece[:, width:]], 1)
        rows = lax.dynamic_update_slice_in_dim(rows, kept, at, 0)

    half = quarter // 2
    up = shift(far[:, :half], "x", 1)
    down = shift(far[:, half:], "x", -1)
    near_up, near_down, own = parts_of(at_x, hiddens, downs)
    up = jnp.concatenate([add(near_up[:, :half], up), near_up[:, half:]], 1).astype(BF)
    up = shift(up, "x", 1)
    down = jnp.concatenate([near_down[:, :half], add(near_down[:, half:], down)], 1)
    down = shift(down.astype(BF), "x", -1)
    summed = own + up.astype(F32) + down.astype(F32)

    def swap(array, *more):
        mine = lax.dynamic_slice_in_dim(array, core * eighth, eighth, 1)
        theirs = lax.dynamic_slice_in_dim(array, (1 - core) * eighth, eighth, 1)
        mine, theirs = (jnp.concatenate([part, *more], 1) for part in (mine, theirs))
        return jnp.concatenate([mine, shift(theirs, "core", 1)], 0)

    residual = swap(rows[:, :quarter], rows[:, quarter:])
    dest = residual[:, eighth].astype(jnp.int32)
    residual = residual[:, :eighth]

    index = jnp.arange(total, dtype=jnp.int32)
    place_z = (index // rows_each) % Z
    behind = jnp.zeros_like(index)
    for i, k in enumerate(ORDER):
        behind = jnp.where(place_z == i, k, behind)
    source_core = jnp.where(index < total // CORES, core, 1 - core)
    source_x = (index // (rows_each * Z)) % X
    source = source_x * Z + lax.rem(z + Z - behind, Z)
    key = (source * CORES + source_core) * rows_each + index % rows_each
    earlier = (dest[:, None] == dest[None, :]) & (key[None, :] < key[:, None])
    rank = jnp.sum(earlier.astype(jnp.int32), axis=1)

    summed = swap(summed).astype(BF)

    slots = X * CORES * SLOTS
    dest_z = (dest // CORES) % Z
    slot_of = ((dest // (CORES * Z)) * CORES + dest % CORES) * SLOTS + rank
    slot = jnp.arange(slots, dtype=jnp.int32)

    def pick(k):
        at = lax.rem(z + k, Z)
        return ((slot_of[None, :] == slot[:, None]) & (dest_z == at)[None, :]).astype(BF)

    def slotted(k):
        return jnp.dot(pick(k), summed, preferred_element_type=F32)

    def message(*steps):
        return jnp.concatenate([slotted(k % Z).astype(BF) for k in steps], 0)

    middle = slots // 2
    up_near = shift(message(3, 1), "z", 1)
    down_near = shift(message(-3, -1), "z", -1)
    opposite = message(4)
    up_far = shift(opposite[:middle], "z", 2)
    down_far = shift(opposite[middle:], "z", -2)
    up = add(slotted(2), up_near[:slots])
    up = jnp.concatenate([add(up[:middle], up_far), up[middle:]], 0)
    down = add(slotted(6), down_near[:slots])
    down = jnp.concatenate([down[:middle], add(down[middle:], down_far)], 0)
    up = shift(up.astype(BF), "z", 2)
    down = shift(down.astype(BF), "z", -2)
    mine = slotted(0) + jnp.dot(pick(0), residual, preferred_element_type=F32)
    near = add(up_near[slots:], down_near[slots:])
    mixed = (mine + near + add(up, down)).astype(BF)

    pieces = lax.all_to_all(
        mixed.reshape(X * CORES, SLOTS, eighth), ("x", "core"), 0, 0, tiled=True
    )
    return pieces.transpose(1, 0, 2).reshape(1, SLOTS, width)


def solution(mesh):
    split = Mesh(
        mesh.devices.reshape(SECTIONS, X, Z, CORES), ("section", "x", "z", "core")
    )
    peers = ("x", "z", "core")
    return jax.shard_map(
        body,
        mesh=split,
        in_specs=(
            P("section", peers, None),
            P("section", peers, None),
            P("section", None),
            P("section", peers, None),
            P("section", peers, None),
            P("section", peers, None),
        ),
        out_specs=P("section", peers, None),
        check_vma=False,
    )
```

```python
import jax
import jax.numpy as jnp
from jax import lax
from jax.sharding import Mesh
from jax.sharding import PartitionSpec as P

SLOTS = 16
X, Z, CORES, SECTIONS = 4, 8, 2, 4
LANES = 128
EPSILON = 1e-05
BF, F32 = jnp.bfloat16, jnp.float32
ORDER = (0, 1, 7, 2, 6, 3, 5, 4)


def shift(array, axis, by):
    n = lax.axis_size(axis)
    return lax.ppermute(array, axis, [(i, (i + by) % n) for i in range(n)])


def handoff(rows, by):
    pairs = [
        (s * X + x, ((s + 1) % SECTIONS) * X + (x + by) % X)
        for s in range(SECTIONS)
        for x in range(X)
    ]
    return lax.ppermute(rows, ("section", "x"), pairs)


def gather_z(block):
    up = down = block
    held = {0: block}
    for step in range(1, Z // 2 + 1):
        up = shift(up, "z", 1)
        held[step] = up
        if step < Z // 2:
            down = shift(down, "z", -1)
            held[Z - step] = down
    return [held[k] for k in ORDER]


def add(a, b):
    return a.astype(F32) + b.astype(F32)


def body(carried, destination, norm_gain, w_gate, w_up, w_down):
    width = carried.shape[2]
    x, z, core = lax.axis_index("x"), lax.axis_index("z"), lax.axis_index("core")
    rows_each = carried.shape[1]
    total = rows_each * X * Z * CORES
    quarter, eighth = width // X, width // (X * CORES)

    def pair(own):
        return jnp.concatenate([own, shift(own, "core", 1)], 0)

    gate_mat, up_mat, down_mat = pair(w_gate[0]), pair(w_up[0]), pair(w_down[0])
    down_part = [
        lax.dynamic_slice_in_dim(down_mat, lax.rem(x + k, X) * quarter, quarter, 1)
        for k in range(X)
    ]

    came = [handoff(carried[0], k) for k in range(X)]
    line = [lax.select_n(lax.rem(x + X - j, X), *came) for j in range(X)]
    dest = jnp.broadcast_to(destination[0].astype(BF), (rows_each, LANES))
    dest = jnp.concatenate([dest, jnp.zeros(((X - 1) * rows_each, LANES), BF)], 0)
    held = gather_z(jnp.concatenate([jnp.concatenate(line, 0), dest], 1))
    dest = jnp.stack([block[:rows_each, width:] for block in held])
    rows = jnp.concatenate([block[:, :width] for block in held], 0)

    gain = norm_gain[0].astype(F32)
    contract = (((1,), (1,)), ((), ()))
    floated = rows.astype(F32)
    scale = lax.rsqrt(jnp.mean(floated * floated, axis=-1, keepdims=True) + EPSILON)
    normed = (floated * scale * gain).astype(BF)
    gate = lax.dot_general(normed, gate_mat, contract, preferred_element_type=F32)
    up = lax.dot_general(normed, up_mat, contract, preferred_element_type=F32)
    hidden = (jax.nn.silu(gate) * up).astype(BF)

    def part(k):
        return jnp.dot(hidden, down_part[k], preferred_element_type=F32)

    half = quarter // 2
    far = part(2).astype(BF)
    up = shift(far[:, :half], "x", 1)
    down = shift(far[:, half:], "x", -1)
    near = part(1)
    up, dest = lax.optimization_barrier((up, dest))
    up = jnp.concatenate([add(near[:, :half], up), near[:, half:]], 1).astype(BF)
    up = shift(up, "x", 1)
    near = part(3)
    down = jnp.concatenate([near[:, :half], add(near[:, half:], down)], 1).astype(BF)
    down = shift(down, "x", -1)
    summed = part(0) + up.astype(F32) + down.astype(F32)

    def swap(array):
        mine = lax.dynamic_slice_in_dim(array, core * eighth, eighth, 1)
        theirs = lax.dynamic_slice_in_dim(array, (1 - core) * eighth, eighth, 1)
        return jnp.concatenate([mine, shift(theirs, "core", 1)], 0)

    residual = swap(lax.dynamic_slice_in_dim(rows, x * quarter, quarter, 1))

    dests = jnp.zeros((X,) + dest.shape, BF)
    for k in range(X):
        there = shift(dest, "x", k) if k else dest
        dests = lax.dynamic_update_slice(
            dests, there[None], (lax.rem(x + X - k, X), 0, 0, 0)
        )
    dests = dests.transpose(1, 0, 2, 3)
    dests = dests.reshape(total // CORES, LANES)
    dest = jnp.concatenate([dests, shift(dests, "core", 1)], 0)[:, 0].astype(jnp.int32)
    index = jnp.arange(total, dtype=jnp.int32)
    block = (index // (X * rows_each)) % Z
    behind = jnp.zeros_like(block)
    for i, k in enumerate(ORDER):
        behind = jnp.where(block == i, k, behind)
    source_core = jnp.where(index < total // CORES, core, 1 - core)
    source = ((index // rows_each) % X) * Z + lax.rem(z + Z - behind, Z)
    key = (source * CORES + source_core) * rows_each + index % rows_each
    earlier = (dest[:, None] == dest[None, :]) & (key[None, :] < key[:, None])
    rank = jnp.sum(earlier.astype(jnp.int32), axis=1)

    summed = swap(summed).astype(BF)

    slots = X * CORES * SLOTS
    dest_z = (dest // CORES) % Z
    slot_of = ((dest // (CORES * Z)) * CORES + dest % CORES) * SLOTS + rank
    slot = jnp.arange(slots, dtype=jnp.int32)

    def pick(k):
        at = lax.rem(z + k, Z)
        return ((slot_of[None, :] == slot[:, None]) & (dest_z == at)[None, :]).astype(BF)

    def slotted(k):
        return jnp.dot(pick(k), summed, preferred_element_type=F32)

    def message(*steps):
        return jnp.concatenate([slotted(k % Z).astype(BF) for k in steps], 0)

    middle = slots // 2
    up_near = shift(message(3, 1), "z", 1)
    down_near = shift(message(-3, -1), "z", -1)
    opposite = message(4)
    up_far = shift(opposite[:middle], "z", 2)
    down_far = shift(opposite[middle:], "z", -2)
    up = add(slotted(2), up_near[:slots])
    up = jnp.concatenate([add(up[:middle], up_far), up[middle:]], 0)
    down = add(slotted(6), down_near[:slots])
    down = jnp.concatenate([down[:middle], add(down[middle:], down_far)], 0)
    up = shift(up.astype(BF), "z", 2)
    down = shift(down.astype(BF), "z", -2)
    mine = slotted(0) + jnp.dot(pick(0), residual, preferred_element_type=F32)
    near = add(up_near[slots:], down_near[slots:])
    mixed = (mine + near + add(up, down)).astype(BF)

    pieces = lax.all_to_all(
        mixed.reshape(X * CORES, SLOTS, eighth), ("x", "core"), 0, 0, tiled=True
    )
    return pieces.transpose(1, 0, 2).reshape(1, SLOTS, width)


def solution(mesh):
    split = Mesh(
        mesh.devices.reshape(SECTIONS, X, Z, CORES), ("section", "x", "z", "core")
    )
    peers = ("x", "z", "core")
    return jax.shard_map(
        body,
        mesh=split,
        in_specs=(
            P("section", peers, None),
            P("section", peers, None),
            P("section", None),
            P("section", peers, None),
            P("section", peers, None),
            P("section", peers, None),
        ),
        out_specs=P("section", peers, None),
        check_vma=False,
    )
```

```python
import jax
import jax.numpy as jnp
from jax import lax
from jax.sharding import Mesh
from jax.sharding import PartitionSpec as P

SLOTS = 16
X, Z, CORES, SECTIONS = 4, 8, 2, 4
LANES = 128
EPSILON = 1e-05
BF, F32 = jnp.bfloat16, jnp.float32
ORDER = (0, 1, 7, 2, 6, 3, 5)


def shift(array, axis, by):
    n = lax.axis_size(axis)
    return lax.ppermute(array, axis, [(i, (i + by) % n) for i in range(n)])


def handoff(rows, by):
    pairs = [
        (s * X + x, ((s + 1) % SECTIONS) * X + (x + by) % X)
        for s in range(SECTIONS)
        for x in range(X)
    ]
    return lax.ppermute(rows, ("section", "x"), pairs)


def gather_z(block):
    up = down = block
    held = {0: block}
    for step in range(1, Z // 2):
        up, down = shift(up, "z", 1), shift(down, "z", -1)
        held[step], held[Z - step] = up, down
    half = block.shape[0] // 2
    far_up, far_down = shift(up[:half], "z", 1), shift(down[half:], "z", -1)
    return [held[k] for k in ORDER] + [far_up, far_down]


def add(a, b):
    return a.astype(F32) + b.astype(F32)


def body(carried, destination, norm_gain, w_gate, w_up, w_down):
    width = carried.shape[2]
    x, z, core = lax.axis_index("x"), lax.axis_index("z"), lax.axis_index("core")
    rows_each = carried.shape[1]
    total = rows_each * X * Z * CORES
    quarter, eighth = width // X, width // (X * CORES)

    def pair(own):
        return jnp.concatenate([own, shift(own, "core", 1)], 0)

    gate_mat, up_mat, down_mat = pair(w_gate[0]), pair(w_up[0]), pair(w_down[0])
    down_part = [
        lax.dynamic_slice_in_dim(down_mat, lax.rem(x + k, X) * quarter, quarter, 1)
        for k in range(X)
    ]

    came = [handoff(carried[0], k) for k in range(X)]
    line = [lax.select_n(lax.rem(x + X - j, X), *came) for j in range(X)]
    dest = jnp.broadcast_to(destination[0].astype(BF), (rows_each, LANES))
    dest = jnp.concatenate([dest, jnp.zeros(((X - 1) * rows_each, LANES), BF)], 0)
    held = gather_z(jnp.concatenate([jnp.concatenate(line, 0), dest], 1))
    dest = jnp.stack([block[:rows_each, width:] for block in held[:-1]])
    rows = jnp.concatenate([block[:, :width] for block in held], 0)

    gain = norm_gain[0].astype(F32)
    contract = (((1,), (1,)), ((), ()))
    floated = rows.astype(F32)
    scale = lax.rsqrt(jnp.mean(floated * floated, axis=-1, keepdims=True) + EPSILON)
    normed = (floated * scale * gain).astype(BF)
    gate = lax.dot_general(normed, gate_mat, contract, preferred_element_type=F32)
    up = lax.dot_general(normed, up_mat, contract, preferred_element_type=F32)
    hidden = (jax.nn.silu(gate) * up).astype(BF)

    def part(k):
        return jnp.dot(hidden, down_part[k], preferred_element_type=F32)

    half = quarter // 2
    far = part(2).astype(BF)
    up = shift(far[:, :half], "x", 1)
    down = shift(far[:, half:], "x", -1)
    near = part(1)
    up, dest = lax.optimization_barrier((up, dest))
    up = jnp.concatenate([add(near[:, :half], up), near[:, half:]], 1).astype(BF)
    up = shift(up, "x", 1)
    near = part(3)
    down = jnp.concatenate([near[:, :half], add(near[:, half:], down)], 1).astype(BF)
    down = shift(down, "x", -1)
    summed = part(0) + up.astype(F32) + down.astype(F32)

    def swap(array):
        mine = lax.dynamic_slice_in_dim(array, core * eighth, eighth, 1)
        theirs = lax.dynamic_slice_in_dim(array, (1 - core) * eighth, eighth, 1)
        return jnp.concatenate([mine, shift(theirs, "core", 1)], 0)

    residual = swap(lax.dynamic_slice_in_dim(rows, x * quarter, quarter, 1))

    dests = jnp.zeros((X,) + dest.shape, BF)
    for k in range(X):
        there = shift(dest, "x", k) if k else dest
        dests = lax.dynamic_update_slice(
            dests, there[None], (lax.rem(x + X - k, X), 0, 0, 0)
        )
    dests = dests.transpose(1, 0, 2, 3)
    dests = dests.reshape(total // CORES, LANES)
    dest = jnp.concatenate([dests, shift(dests, "core", 1)], 0)[:, 0].astype(jnp.int32)
    index = jnp.arange(total, dtype=jnp.int32)
    block = (index // (X * rows_each)) % Z
    behind = jnp.zeros_like(block)
    for i, k in enumerate(ORDER + (Z // 2,)):
        behind = jnp.where(block == i, k, behind)
    source_core = jnp.where(index < total // CORES, core, 1 - core)
    source = ((index // rows_each) % X) * Z + lax.rem(z + Z - behind, Z)
    key = (source * CORES + source_core) * rows_each + index % rows_each
    earlier = (dest[:, None] == dest[None, :]) & (key[None, :] < key[:, None])
    rank = jnp.sum(earlier.astype(jnp.int32), axis=1)

    summed = swap(summed).astype(BF)

    slots = X * CORES * SLOTS
    dest_z = (dest // CORES) % Z
    slot_of = ((dest // (CORES * Z)) * CORES + dest % CORES) * SLOTS + rank
    slot = jnp.arange(slots, dtype=jnp.int32)

    def pick(k):
        at = lax.rem(z + k, Z)
        return ((slot_of[None, :] == slot[:, None]) & (dest_z == at)[None, :]).astype(BF)

    def slotted(k):
        return jnp.dot(pick(k), summed, preferred_element_type=F32)

    middle = slots // 2
    far = slotted(Z // 2).astype(BF)
    up, down = shift(far[:middle], "z", 1), shift(far[middle:], "z", -1)
    for k in range(Z // 2 - 1, 0, -1):
        above, below = slotted(k), slotted(Z - k)
        if k == Z // 2 - 1:
            up = jnp.concatenate([add(above[:middle], up), above[middle:]], 0)
            down = jnp.concatenate([below[:middle], add(below[middle:], down)], 0)
        else:
            up, down = add(above, up), add(below, down)
        up, down = shift(up.astype(BF), "z", 1), shift(down.astype(BF), "z", -1)
    mine = slotted(0) + jnp.dot(pick(0), residual, preferred_element_type=F32)
    mixed = (mine + add(up, down)).astype(BF)

    mixed = mixed.reshape(X, CORES, SLOTS, eighth)
    mine = lax.dynamic_index_in_dim(mixed, core, 1, keepdims=False)
    theirs = lax.dynamic_index_in_dim(mixed, 1 - core, 1, keepdims=False)
    theirs = shift(theirs, "core", 1)
    pair = [jnp.where(core == 0, mine, theirs), jnp.where(core == 0, theirs, mine)]
    pair = jnp.concatenate(pair, -1)
    came = [
        lax.dynamic_index_in_dim(pair, lax.rem(x + k, X), 0, keepdims=False) for k in range(X)
    ]
    came = [came[0]] + [shift(came[k], "x", k) for k in range(1, X)]
    return jnp.concatenate(
        [lax.select_n(lax.rem(x + X - j, X), *came) for j in range(X)], -1
    )[None]


def solution(mesh):
    split = Mesh(
        mesh.devices.reshape(SECTIONS, X, Z, CORES), ("section", "x", "z", "core")
    )
    peers = ("x", "z", "core")
    return jax.shard_map(
        body,
        mesh=split,
        in_specs=(
            P("section", peers, None),
            P("section", peers, None),
            P("section", None),
            P("section", peers, None),
            P("section", peers, None),
            P("section", peers, None),
        ),
        out_specs=P("section", peers, None),
        check_vma=False,
    )
```

```python
import jax
import jax.numpy as jnp
from jax import lax
from jax.sharding import Mesh
from jax.sharding import PartitionSpec as P

SLOTS = 16
X, Z, CORES, SECTIONS = 4, 8, 2, 4
LANES = 128
EPSILON = 1e-05
BF, F32 = jnp.bfloat16, jnp.float32
ORDER = (0, 1, 7, 2, 6, 3, 5)


def shift(array, axis, by):
    n = lax.axis_size(axis)
    return lax.ppermute(array, axis, [(i, (i + by) % n) for i in range(n)])


def handoff(rows, by):
    pairs = [
        (s * X + x, ((s + 1) % SECTIONS) * X + (x + by) % X)
        for s in range(SECTIONS)
        for x in range(X)
    ]
    return lax.ppermute(rows, ("section", "x"), pairs)


def gather_z(block):
    up = down = block
    held = {0: block}
    for step in range(1, Z // 2):
        up, down = shift(up, "z", 1), shift(down, "z", -1)
        held[step], held[Z - step] = up, down
    half = block.shape[0] // 2
    far_up, far_down = shift(up[:half], "z", 1), shift(down[half:], "z", -1)
    return [held[k] for k in ORDER] + [far_up, far_down]


def add(a, b):
    return a.astype(F32) + b.astype(F32)


def body(carried, destination, norm_gain, w_gate, w_up, w_down):
    width = carried.shape[2]
    x, z, core = lax.axis_index("x"), lax.axis_index("z"), lax.axis_index("core")
    rows_each = carried.shape[1]
    total = rows_each * X * Z * CORES
    quarter, eighth = width // X, width // (X * CORES)

    def pair(own):
        return jnp.concatenate([own, shift(own, "core", 1)], 0)

    gate_mat, up_mat, down_mat = pair(w_gate[0]), pair(w_up[0]), pair(w_down[0])
    down_part = [
        lax.dynamic_slice_in_dim(down_mat, lax.rem(x + k, X) * quarter, quarter, 1)
        for k in range(X)
    ]

    came = [handoff(carried[0], k) for k in range(X)]
    line = [lax.select_n(lax.rem(x + X - j, X), *came) for j in range(X)]
    dest = jnp.broadcast_to(destination[0].astype(BF), (rows_each, LANES))
    dest = jnp.concatenate([dest, jnp.zeros(((X - 1) * rows_each, LANES), BF)], 0)
    held = gather_z(jnp.concatenate([jnp.concatenate(line, 0), dest], 1))
    dest = jnp.stack([block[:rows_each, width:] for block in held[:-1]])
    rows = jnp.concatenate([block[:, :width] for block in held], 0)

    gain = norm_gain[0].astype(F32)
    contract = (((1,), (1,)), ((), ()))
    floated = rows.astype(F32)
    scale = lax.rsqrt(jnp.mean(floated * floated, axis=-1, keepdims=True) + EPSILON)
    normed = (floated * scale * gain).astype(BF)
    gate = lax.dot_general(normed, gate_mat, contract, preferred_element_type=F32)
    up = lax.dot_general(normed, up_mat, contract, preferred_element_type=F32)
    hidden = (jax.nn.silu(gate) * up).astype(BF)

    def part(k):
        return jnp.dot(hidden, down_part[k], preferred_element_type=F32)

    half = quarter // 2
    far = part(2).astype(BF)
    up = shift(far[:, :half], "x", 1)
    down = shift(far[:, half:], "x", -1)
    near = part(1)
    up, dest = lax.optimization_barrier((up, dest))
    up = jnp.concatenate([add(near[:, :half], up), near[:, half:]], 1).astype(BF)
    up = shift(up, "x", 1)
    near = part(3)
    down = jnp.concatenate([near[:, :half], add(near[:, half:], down)], 1).astype(BF)
    down = shift(down, "x", -1)
    summed = part(0) + up.astype(F32) + down.astype(F32)

    def swap(array):
        mine = lax.dynamic_slice_in_dim(array, core * eighth, eighth, 1)
        theirs = lax.dynamic_slice_in_dim(array, (1 - core) * eighth, eighth, 1)
        return jnp.concatenate([mine, shift(theirs, "core", 1)], 0)

    residual = swap(lax.dynamic_slice_in_dim(rows, x * quarter, quarter, 1))

    dests = jnp.zeros((X,) + dest.shape, BF)
    for k in (0, 1, 3, 2):
        there = shift(dest, "x", k) if k else dest
        dests = lax.dynamic_update_slice(
            dests, there[None], (lax.rem(x + X - k, X), 0, 0, 0)
        )
    dests = dests.transpose(1, 0, 2, 3)
    dests = dests.reshape(total // CORES, LANES)
    dest = jnp.concatenate([dests, shift(dests, "core", 1)], 0)[:, 0].astype(jnp.int32)
    index = jnp.arange(total, dtype=jnp.int32)
    block = (index // (X * rows_each)) % Z
    behind = jnp.zeros_like(block)
    for i, k in enumerate(ORDER + (Z // 2,)):
        behind = jnp.where(block == i, k, behind)
    source_core = jnp.where(index < total // CORES, core, 1 - core)
    source = ((index // rows_each) % X) * Z + lax.rem(z + Z - behind, Z)
    key = (source * CORES + source_core) * rows_each + index % rows_each
    earlier = (dest[:, None] == dest[None, :]) & (key[None, :] < key[:, None])
    rank = jnp.sum(earlier.astype(jnp.int32), axis=1)

    summed = swap(summed).astype(BF)

    slots = X * CORES * SLOTS
    dest_z = (dest // CORES) % Z
    slot_of = ((dest // (CORES * Z)) * CORES + dest % CORES) * SLOTS + rank
    slot = jnp.arange(slots, dtype=jnp.int32)

    def pick(k):
        at = lax.rem(z + k, Z)
        return ((slot_of[None, :] == slot[:, None]) & (dest_z == at)[None, :]).astype(BF)

    def slotted(k):
        return jnp.dot(pick(k), summed, preferred_element_type=F32)

    middle = slots // 2
    far = slotted(Z // 2).astype(BF)
    up, down = shift(far[:middle], "z", 1), shift(far[middle:], "z", -1)
    for k in range(Z // 2 - 1, 0, -1):
        above, below = slotted(k), slotted(Z - k)
        if k == Z // 2 - 1:
            up = jnp.concatenate([add(above[:middle], up), above[middle:]], 0)
            down = jnp.concatenate([below[:middle], add(below[middle:], down)], 0)
        else:
            up, down = add(above, up), add(below, down)
        up, down = shift(up.astype(BF), "z", 1), shift(down.astype(BF), "z", -1)
    mine = slotted(0) + jnp.dot(pick(0), residual, preferred_element_type=F32)
    mixed = (mine + add(up, down)).astype(BF)

    mixed = mixed.reshape(X, CORES, SLOTS, eighth)
    mine = lax.dynamic_index_in_dim(mixed, core, 1, keepdims=False)
    theirs = lax.dynamic_index_in_dim(mixed, 1 - core, 1, keepdims=False)
    theirs = shift(theirs, "core", 1)
    pair = [jnp.where(core == 0, mine, theirs), jnp.where(core == 0, theirs, mine)]
    pair = jnp.concatenate(pair, -1)
    came = [
        lax.dynamic_index_in_dim(pair, lax.rem(x + k, X), 0, keepdims=False) for k in range(X)
    ]
    came = [came[0]] + [shift(came[k], "x", k) for k in range(1, X)]
    return jnp.concatenate(
        [lax.select_n(lax.rem(x + X - j, X), *came) for j in range(X)], -1
    )[None]


def solution(mesh):
    split = Mesh(
        mesh.devices.reshape(SECTIONS, X, Z, CORES), ("section", "x", "z", "core")
    )
    peers = ("x", "z", "core")
    return jax.shard_map(
        body,
        mesh=split,
        in_specs=(
            P("section", peers, None),
            P("section", peers, None),
            P("section", None),
            P("section", peers, None),
            P("section", peers, None),
            P("section", peers, None),
        ),
        out_specs=P("section", peers, None),
        check_vma=False,
    )
```
